32 devices in a mesh: ctx: 8 (over z, x), head: 4 (over y, core).
Axes of the slice: x: 2, y: 2, z: 4, core: 2. Of those that a mesh axis runs over, the one named last changes fastest.
Arguments:
- queries: bfloat16 [8192, 4, 4, 128], P('ctx', None, 'head'), may hold values from -4.5 to 4.5
- key_rows: bfloat16 [8192, 4, 128], P('ctx'), may hold values from -3 to 3
- value_rows: bfloat16 [8192, 4, 128], P('ctx'), may hold values from -6 to 6
- out_grad: bfloat16 [8192, 4, 4, 128], P('ctx', None, 'head'), may hold values from -18 to 18
- outputs: bfloat16 [8192, 4, 4, 128], P('ctx', None, 'head'), may hold values from -6 to 6
- logsumexp: float32 [4, 4, 8192], P(None, 'head', 'ctx'), as said below
- selections: int32 [64, 3], P('ctx'), may hold values from 0 to 7, as said below
Outputs:
- grad_queries: bfloat16 [8192, 4, 4, 128], P('ctx', None, 'head')
- grad_keys: bfloat16 [8192, 4, 128], P('ctx', 'head')
- grad_values: bfloat16 [8192, 4, 128], P('ctx', 'head')
The draws below stay inside these ranges and needn't reach their ends.
Inputs may be any that keep to these rules, and one draw needn't show every extreme that they name: `selections`: column 0 of row b is the query block's own key block b // 8; columns 1 and 2 each name an earlier key block or repeat the own block, and two earlier blocks in one row differ. The query blocks of one key block never name the same earlier block twice. For every key block after the first, exactly one of its query blocks names key block 0. `logsumexp`: the log-sum-exp of scores over each query's attended keys, computed from queries and key_rows as in the reference program.
All inputs are finite; a program needn't handle non-finite values.
Results may differ from the reference program's by a relative error of at most 0.005.
Values may be sent and summed in bfloat16 or wider, within the bound.
A program may use at most 128 MiB of HBM per device.

```python
import jax
import jax.numpy as jnp
from jax import lax

CTX_DEV = 1024
QB = 128
KV = 4
GROUP = 4
HD = 128
TOKENS = 8192
NQB = 64


def moba_rows(base_key, shape, bound):
    return jnp.clip(jax.random.normal(base_key, shape, jnp.float32), -3.0, 3.0) * (bound / 3.0)


def moba_queries(base_key):
    return moba_rows(jax.random.fold_in(base_key, 11), (TOKENS, KV, GROUP, HD), 4.5).astype(jnp.bfloat16)


def moba_keys(base_key):
    return moba_rows(jax.random.fold_in(base_key, 12), (TOKENS, KV, HD), 3.0).astype(jnp.bfloat16)


def moba_selections(base_key):
    table_key = jax.random.fold_in(base_key, 13)
    first_key, second_key = jax.random.split(table_key)
    block_count = TOKENS // CTX_DEV
    per_block = CTX_DEV // QB
    raw = jax.random.randint(first_key, (block_count, block_count), 0, 2 ** 20)
    columns = jnp.arange(block_count, dtype=jnp.int32)[None, :]
    rows_idx = jnp.arange(block_count, dtype=jnp.int32)[:, None]
    score = raw * block_count + columns
    score = jnp.where(columns == 0, -1, score)
    score = jnp.where(columns >= rows_idx, 2 ** 30, score)
    ordering = jnp.argsort(score, axis=1).astype(jnp.int32)
    offsets = jax.random.randint(second_key, (block_count,), 0, per_block)
    query_ids = jnp.arange(block_count * per_block, dtype=jnp.int32)
    owner = query_ids // per_block
    within = query_ids % per_block
    place = (within + offsets[owner]) % per_block

    def pick(position):
        safe = jnp.minimum(position, block_count - 1)
        return jnp.where(position < owner, ordering[owner, safe], owner)
    return jnp.stack([owner, pick(2 * place), pick(2 * place + 1)], axis=1).astype(jnp.int32)


def moba_logsumexp(base_key):
    queries = moba_queries(base_key).astype(jnp.float32)
    key_rows = moba_keys(base_key).astype(jnp.float32)
    chosen_all = moba_selections(base_key)
    scale = HD ** (-0.5)

    def one_block(block_idx):
        first = (block_idx * QB).astype(jnp.int32)
        q_blk = lax.dynamic_slice_in_dim(queries, first, QB, 0)
        chosen = chosen_all[block_idx]
        valid = jnp.stack([chosen[0] == chosen[0], chosen[1] != chosen[0], (chosen[2] != chosen[0]) & (chosen[2] != chosen[1])])
        starts = (chosen * CTX_DEV).astype(jnp.int32)
        key_sel = jnp.stack([lax.dynamic_slice_in_dim(key_rows, starts[j], CTX_DEV, 0) for j in range(3)])
        q_pos = first + jnp.arange(QB, dtype=jnp.int32)
        k_pos = starts[:, None] + jnp.arange(CTX_DEV, dtype=jnp.int32)[None, :]
        allowed = valid[None, :, None] & (k_pos[None, :, :] <= q_pos[:, None, None])
        scores = jnp.einsum('qkgd,jckd->kgqjc', q_blk, key_sel) * scale
        masked = jnp.where(allowed, scores, -1e+30)
        top = jnp.max(masked, axis=(3, 4), keepdims=True)
        total = jnp.sum(jnp.where(allowed, jnp.exp(masked - top), 0.0), axis=(3, 4))
        return top[:, :, :, 0, 0] + jnp.log(total)
    stacked = lax.map(one_block, jnp.arange(NQB, dtype=jnp.int32))
    return jnp.transpose(stacked, (1, 2, 0, 3)).reshape(KV, GROUP, TOKENS)


def draw_queries(key, part):
    return moba_queries(key)


def draw_key_rows(key, part):
    return moba_keys(key)


def draw_selections(key, part):
    return moba_selections(key)


def draw_logsumexp(key, part):
    return moba_logsumexp(key).astype(jnp.float32)


def block_levels(rng, shape, cuts, smallest, top_value):
    level = 1.0
    for dim, blocks in cuts:
        heights = jax.random.uniform(jax.random.fold_in(jax.random.fold_in(rng, 6), dim), (blocks,), jnp.float32, smallest / len(cuts), top_value / len(cuts))
        level = level * jnp.repeat(jnp.exp(heights), shape[dim] // blocks).reshape((-1,) + (1,) * (len(shape) - 1 - dim))
    return level


def noise(key, extent, width, most, cuts=(), held_as=jnp.bfloat16):
    array = width * jax.random.normal(key, extent, jnp.float32)
    if cuts:
        array = array * block_levels(key, extent, cuts, -0.22, 0.18)
    return jnp.clip(array, -most, most).astype(held_as)


def setup_inputs(seed: int = 0) -> dict:
    key_list = jax.random.split(jax.random.key(seed), 8)
    queries = draw_queries(jax.random.fold_in(key_list[7], 71), 0)
    key_rows = draw_key_rows(jax.random.fold_in(key_list[7], 71), 0)
    value_rows = noise(key_list[2], (TOKENS, KV, HD), 1.0, 6.0, ((0, 8),))
    out_grad = noise(key_list[3], (TOKENS, KV, GROUP, HD), 3.0, 18.0, ((0, 8), (2, 4)))
    outputs = noise(key_list[4], (TOKENS, KV, GROUP, HD), 1.0, 6.0, ((0, 8), (2, 4)))
    logsumexp = draw_logsumexp(jax.random.fold_in(key_list[7], 71), 0)
    selections = draw_selections(jax.random.fold_in(key_list[7], 71), 0)
    return {"queries": queries, "key_rows": key_rows, "value_rows": value_rows, "out_grad": out_grad, "outputs": outputs, "logsumexp": logsumexp, "selections": selections}


def reference(queries, key_rows, value_rows, out_grad, outputs, logsumexp, selections):
    token_count = queries.shape[0]
    scale = HD ** -0.5
    block_total = token_count // QB
    delta_all = jnp.sum(out_grad.astype(jnp.float32) * outputs.astype(jnp.float32), axis=-1)
    zero_rows = jnp.zeros(key_rows.shape, jnp.float32)

    def one_block(carry, block_idx):
        grad_k, grad_v = carry
        first = (block_idx * QB).astype(jnp.int32)
        q_blk = lax.dynamic_slice_in_dim(queries, first, QB, 0).astype(jnp.float32)
        g_blk = lax.dynamic_slice_in_dim(out_grad, first, QB, 0).astype(jnp.float32)
        lse_blk = lax.dynamic_slice_in_dim(logsumexp, first, QB, 2)
        delta_blk = jnp.transpose(lax.dynamic_slice_in_dim(delta_all, first, QB, 0), (1, 2, 0))
        chosen = selections[block_idx]
        valid = jnp.stack([chosen[0] == chosen[0], chosen[1] != chosen[0], (chosen[2] != chosen[0]) & (chosen[2] != chosen[1])])
        starts = (chosen * CTX_DEV).astype(jnp.int32)
        key_sel = jnp.stack([lax.dynamic_slice_in_dim(key_rows, starts[j], CTX_DEV, 0) for j in range(3)]).astype(jnp.float32)
        value_sel = jnp.stack([lax.dynamic_slice_in_dim(value_rows, starts[j], CTX_DEV, 0) for j in range(3)]).astype(jnp.float32)
        q_pos = first + jnp.arange(QB, dtype=jnp.int32)
        k_pos = starts[:, None] + jnp.arange(CTX_DEV, dtype=jnp.int32)[None, :]
        allowed = valid[None, :, None] & (k_pos[None, :, :] <= q_pos[:, None, None])
        scores = jnp.einsum('qkgd,jckd->kgqjc', q_blk, key_sel) * scale
        prob = jnp.where(allowed, jnp.exp(scores - lse_blk[..., None, None]), 0.0)
        dprob = jnp.einsum('qkgd,jckd->kgqjc', g_blk, value_sel)
        dscore = prob * (dprob - delta_blk[..., None, None])
        prob_low = lax.optimization_barrier(prob.astype(jnp.bfloat16)).astype(jnp.float32)
        dscore_low = lax.optimization_barrier(dscore.astype(jnp.bfloat16)).astype(jnp.float32)
        grad_q = jnp.einsum('kgqjc,jckd->qkgd', dscore_low, key_sel) * scale
        part_k = jnp.einsum('kgqjc,qkgd->jckd', dscore_low, q_blk) * scale
        part_v = jnp.einsum('kgqjc,qkgd->jckd', prob_low, g_blk)
        for j in range(3):
            old_k = lax.dynamic_slice_in_dim(grad_k, starts[j], CTX_DEV, 0)
            grad_k = lax.dynamic_update_slice_in_dim(grad_k, old_k + part_k[j], starts[j], 0)
            old_v = lax.dynamic_slice_in_dim(grad_v, starts[j], CTX_DEV, 0)
            grad_v = lax.dynamic_update_slice_in_dim(grad_v, old_v + part_v[j], starts[j], 0)
        return (grad_k, grad_v), grad_q.astype(jnp.bfloat16)

    (grad_k, grad_v), grad_q = lax.scan(one_block, (zero_rows, zero_rows), jnp.arange(block_total, dtype=jnp.int32))
    return grad_q.reshape(queries.shape), grad_k.astype(jnp.bfloat16), grad_v.astype(jnp.bfloat16)
```

```python
import functools
import math

import jax
import jax.numpy as jnp
from jax import lax
from jax.experimental import pallas as pl
from jax.experimental.pallas import tpu as pltpu
from jax.sharding import PartitionSpec as P

QB = 128
TILE = 256
DEAD = 1e30
LOG2E = math.log2(math.e)
NT = (((1,), (1,)), ((), ()))
VMEM_LIMIT = 48 * 1024 * 1024


def dot(a, b, dims=(((1,), (0,)), ((), ()))):
    return lax.dot_general(a, b, dims, preferred_element_type=jnp.float32)


def piece(k, k_t, v, q, g, lse2, delta, scale, causal=False):
    p = jnp.exp2(dot(k, q, NT) * (scale * LOG2E) - lse2)
    if causal:
        keep = lax.broadcasted_iota(jnp.int32, p.shape, 0) <= lax.broadcasted_iota(
            jnp.int32, p.shape, 1
        )
        p = jnp.where(keep, p, 0.0)
    ds = (p * (dot(v, g, NT) - delta)).astype(jnp.bfloat16)
    return dot(k_t, ds), dot(ds, q), dot(p.astype(jnp.bfloat16), g)


def pick_kernel(source_ref, live_ref, q_ref, g_ref, stat_ref, q_out, g_out, stat_out):
    rows = stat_ref.shape[1]
    for peer in range(q_out.shape[0]):
        block = source_ref[peer]
        q_out[peer] = q_ref[block]
        g_out[peer] = g_ref[block]
        stat_out[peer, :rows] = stat_ref[block]
        live = live_ref[peer].astype(jnp.float32)
        stat_out[peer, rows:] = jnp.full((stat_out.shape[1] - rows, QB), live, jnp.float32)


def own_kernel(scale, q_ref, g_ref, k_ref, v_ref, lse_ref, delta_ref, dq_ref, dk_ref, dv_ref):
    rows = q_ref.shape[0]
    k_t = k_ref[...].T
    for lo in range(0, rows, TILE):
        here = pl.ds(lo, TILE)
        q, g = q_ref[here, :], g_ref[here, :]
        lse2, delta = lse_ref[0, :, here] * LOG2E, delta_ref[0, :, here]
        dq, dk, dv = piece(
            k_ref[here, :], k_t[:, lo : lo + TILE], v_ref[here, :], q, g, lse2, delta, scale, True
        )
        dk_ref[here, :] = dk
        dv_ref[here, :] = dv
        if lo:
            dq_more, dk, dv = piece(
                k_ref[:lo, :], k_t[:, :lo], v_ref[:lo, :], q, g, lse2, delta, scale
            )
            dq += dq_more
            dk_ref[:lo, :] += dk
            dv_ref[:lo, :] += dv
        dq_ref[here, :] = dq.T * scale


def slots_kernel(
    scale, mark_ref, q_ref, g_ref, stat_ref, k_ref, v_ref, dk_in, dv_in, dq_ref, dk_ref, dv_ref,
    acc_k, acc_v,
):
    head = pl.program_id(0)
    heads = pl.num_programs(0)
    k_t = k_ref[...].T
    acc_k[...] = dk_in[...]
    acc_v[...] = dv_in[...]
    for slot in range(q_ref.shape[0] // QB):
        here = pl.ds(slot * QB, QB)

        @pl.when(mark_ref[slot] > 0)
        def _():
            q, g = q_ref[here, :], g_ref[here, :]
            lse2 = stat_ref[slot, pl.ds(head, 1), :] * LOG2E
            delta = stat_ref[slot, pl.ds(heads + head, 1), :]
            dq, dk, dv = piece(k_ref[...], k_t, v_ref[...], q, g, lse2, delta, scale)
            acc_k[...] += dk
            acc_v[...] += dv
            dq_ref[here, :] = (dq.T * scale).astype(dq_ref.dtype)

        @pl.when(mark_ref[slot] <= 0)
        def _():
            dq_ref[here, :] = jnp.zeros((QB, q_ref.shape[1]), dq_ref.dtype)

    dk_ref[0] = (acc_k[...] * scale).astype(dk_ref.dtype)
    dv_ref[0] = acc_v[...].astype(dv_ref.dtype)


def merge_kernel(first_ref, second_ref, own_ref, back_ref, out_ref):
    for block in range(own_ref.shape[0] // QB):
        here = pl.ds(block * QB, QB)
        total = own_ref[here, :]
        for pick_ref in (first_ref, second_ref):
            pick = pick_ref[block]
            part = back_ref[jnp.maximum(pick, 0)].astype(jnp.float32)
            total += jnp.where(pick >= 0, part, 0.0)
        out_ref[here, :] = total.astype(out_ref.dtype)


def body(queries, key_rows, value_rows, out_grad, outputs, logsumexp, selections):
    rows, kv, local, hd = queries.shape
    width = kv * local * hd
    heads = kv * local
    blocks = rows // QB
    peers = lax.axis_size("ctx")
    device = lax.axis_index("ctx")
    scale = hd ** (-0.5)
    f32, bf16 = jnp.float32, jnp.bfloat16
    params = pltpu.CompilerParams(vmem_limit_bytes=VMEM_LIMIT)

    q2 = queries.reshape(rows, width)
    g2 = out_grad.reshape(rows, width)
    k2 = key_rows.reshape(rows, kv * hd)
    v2 = value_rows.reshape(rows, kv * hd)
    lse = logsumexp.reshape(heads, rows)
    delta = jnp.transpose(
        jnp.sum((out_grad.astype(f32) * outputs.astype(f32)).reshape(rows, heads, hd), -1)
    )

    peer_ids = jnp.arange(peers, dtype=jnp.int32)
    block_ids = jnp.arange(blocks, dtype=jnp.int32)
    match = jnp.any(selections[:, 1:, None] == peer_ids, axis=1) & (peer_ids != device)
    live = jnp.any(match, axis=0)
    source = jnp.sum(jnp.where(match, block_ids[:, None], 0), axis=0)
    stats = jnp.concatenate([lse, delta], 0).reshape(2 * heads, blocks, QB).transpose(1, 0, 2)
    smem = pl.BlockSpec(memory_space=pltpu.SMEM)
    vmem = pl.BlockSpec(memory_space=pltpu.VMEM)
    q_blocks, g_blocks, send_stat = pl.pallas_call(
        pick_kernel,
        in_specs=[smem, smem, vmem, vmem, vmem],
        out_specs=[vmem] * 3,
        out_shape=[
            jax.ShapeDtypeStruct((peers, QB, width), bf16),
            jax.ShapeDtypeStruct((peers, QB, width), bf16),
            jax.ShapeDtypeStruct((peers, 3 * heads, QB), f32),
        ],
        compiler_params=params,
        name="pick",
    )(
        source,
        live.astype(jnp.int32),
        q2.reshape(blocks, QB, width),
        g2.reshape(blocks, QB, width),
        stats,
    )
    swap = functools.partial(
        lax.all_to_all, axis_name="ctx", split_axis=0, concat_axis=0, tiled=True
    )
    got_stat = swap(send_stat)
    got_q = swap(q_blocks).reshape(peers * QB, width)
    got_g = swap(g_blocks).reshape(peers * QB, width)

    column = lambda n: pl.BlockSpec((n, hd), lambda h, *_: (0, h))
    keys = pl.BlockSpec((rows, hd), lambda h, *_: (0, h // local))
    row = pl.BlockSpec((1, 1, rows), lambda h, *_: (h, 0, 0))
    own_q, own_k, own_v = pl.pallas_call(
        functools.partial(own_kernel, scale),
        grid=(heads,),
        in_specs=[column(rows), column(rows), keys, keys, row, row],
        out_specs=[column(rows)] * 3,
        out_shape=[jax.ShapeDtypeStruct((rows, width), f32)] * 3,
        compiler_params=params,
        name="own",
    )(q2, g2, k2, v2, lse.reshape(heads, 1, rows), delta.reshape(heads, 1, rows))

    marks = (got_stat[:, 2 * heads, 0] > 0).astype(jnp.int32)
    stacked = pl.BlockSpec((1, rows, hd), lambda h, *_: (h, 0, 0))
    dq_out, dk, dv = pl.pallas_call(
        functools.partial(slots_kernel, scale),
        grid_spec=pltpu.PrefetchScalarGridSpec(
            num_scalar_prefetch=1,
            grid=(heads,),
            in_specs=[
                column(peers * QB),
                column(peers * QB),
                pl.BlockSpec(got_stat.shape, lambda h, *_: (0, 0, 0)),
                keys,
                keys,
                column(rows),
                column(rows),
            ],
            out_specs=[column(peers * QB), stacked, stacked],
            scratch_shapes=[pltpu.VMEM((rows, hd), f32)] * 2,
        ),
        out_shape=[
            jax.ShapeDtypeStruct((peers * QB, width), bf16),
            jax.ShapeDtypeStruct((heads, rows, hd), bf16),
            jax.ShapeDtypeStruct((heads, rows, hd), bf16),
        ],
        compiler_params=params,
        name="slots",
    )(marks, got_q, got_g, got_stat, k2, v2, own_k, own_v)

    back = swap(dq_out.reshape(peers, QB, width))
    to_head = functools.partial(
        lax.all_to_all, axis_name="head", split_axis=0, concat_axis=0, tiled=True
    )
    shards = lax.axis_size("head")

    def reduce_heads(part):
        part = to_head(part).reshape(shards, kv // shards, local, rows, hd)
        total = jnp.sum(part.astype(f32), axis=(0, 2))
        return jnp.transpose(total, (1, 0, 2)).astype(bf16)

    first, second = selections[:, 1], selections[:, 2]
    first = jnp.where(first != device, first, -1)
    second = jnp.where((second != device) & (second != first), second, -1)
    grad_q = pl.pallas_call(
        merge_kernel,
        in_specs=[smem, smem, vmem, vmem],
        out_specs=vmem,
        out_shape=jax.ShapeDtypeStruct((rows, width), bf16),
        compiler_params=params,
        name="merge",
    )(first, second, own_q, back)
    return (grad_q.reshape(rows, kv, local, hd), reduce_heads(dk), reduce_heads(dv))


def solution(mesh):
    in_specs = (
        P("ctx", None, "head", None),
        P("ctx", None, None),
        P("ctx", None, None),
        P("ctx", None, "head", None),
        P("ctx", None, "head", None),
        P(None, "head", "ctx"),
        P("ctx", None),
    )
    out_specs = (P("ctx", None, "head", None), P("ctx", "head", None), P("ctx", "head", None))
    return jax.shard_map(body, mesh=mesh, in_specs=in_specs, out_specs=out_specs, check_vma=False)
```

```python
import functools
import math

import jax
import jax.numpy as jnp
from jax import lax
from jax.experimental import pallas as pl
from jax.experimental.pallas import tpu as pltpu
from jax.sharding import PartitionSpec as P

QB = 128
TILE = 256
DEAD = 1e30
LOG2E = math.log2(math.e)
NT = (((1,), (1,)), ((), ()))
VMEM_LIMIT = 48 * 1024 * 1024


def dot(a, b, dims=(((1,), (0,)), ((), ()))):
    return lax.dot_general(a, b, dims, preferred_element_type=jnp.float32)


def piece(k, k_t, v, q, g, lse2, delta, scale, causal=False):
    p = jnp.exp2(dot(k, q, NT) * (scale * LOG2E) - lse2)
    if causal:
        keep = lax.broadcasted_iota(jnp.int32, p.shape, 0) <= lax.broadcasted_iota(
            jnp.int32, p.shape, 1
        )
        p = jnp.where(keep, p, 0.0)
    ds = (p * (dot(v, g, NT) - delta)).astype(jnp.bfloat16)
    return dot(k_t, ds), dot(ds, q), dot(p.astype(jnp.bfloat16), g)


def pick_kernel(source_ref, live_ref, q_ref, g_ref, stat_ref, q_out, g_out, stat_out):
    rows = stat_ref.shape[1]
    for peer in range(q_out.shape[0]):
        block = source_ref[peer]
        q_out[peer] = q_ref[block]
        g_out[peer] = g_ref[block]
        stat_out[peer, :rows] = stat_ref[block]
        live = live_ref[peer].astype(jnp.float32)
        stat_out[peer, rows:] = jnp.full((stat_out.shape[1] - rows, QB), live, jnp.float32)


def own_kernel(scale, q_ref, g_ref, k_ref, v_ref, lse_ref, delta_ref, dq_ref, dk_ref, dv_ref):
    rows = q_ref.shape[0]
    k_t = k_ref[...].T
    for lo in range(0, rows, TILE):
        here = pl.ds(lo, TILE)
        q, g = q_ref[here, :], g_ref[here, :]
        lse2, delta = lse_ref[0, :, here] * LOG2E, delta_ref[0, :, here]
        dq, dk, dv = piece(
            k_ref[here, :], k_t[:, lo : lo + TILE], v_ref[here, :], q, g, lse2, delta, scale, True
        )
        dk_ref[here, :] = dk
        dv_ref[here, :] = dv
        if lo:
            dq_more, dk, dv = piece(
                k_ref[:lo, :], k_t[:, :lo], v_ref[:lo, :], q, g, lse2, delta, scale
            )
            dq += dq_more
            dk_ref[:lo, :] += dk
            dv_ref[:lo, :] += dv
        dq_ref[here, :] = dq.T * scale


def slots_kernel(
    scale, mark_ref, q_ref, g_ref, stat_ref, k_ref, v_ref, dk_in, dv_in, dq_ref, dk_ref, dv_ref,
    acc_k, acc_v,
):
    head = pl.program_id(0)
    heads = pl.num_programs(0)
    k_t = k_ref[...].T
    acc_k[...] = dk_in[...]
    acc_v[...] = dv_in[...]
    for slot in range(q_ref.shape[0] // QB):
        here = pl.ds(slot * QB, QB)

        @pl.when(mark_ref[slot] > 0)
        def _():
            q, g = q_ref[here, :], g_ref[here, :]
            lse2 = stat_ref[slot, pl.ds(head, 1), :] * LOG2E
            delta = stat_ref[slot, pl.ds(heads + head, 1), :]
            dq, dk, dv = piece(k_ref[...], k_t, v_ref[...], q, g, lse2, delta, scale)
            acc_k[...] += dk
            acc_v[...] += dv
            dq_ref[here, :] = (dq.T * scale).astype(dq_ref.dtype)

        @pl.when(mark_ref[slot] <= 0)
        def _():
            dq_ref[here, :] = jnp.zeros((QB, q_ref.shape[1]), dq_ref.dtype)

    dk_ref[0] = (acc_k[...] * scale).astype(dk_ref.dtype)
    dv_ref[0] = acc_v[...].astype(dv_ref.dtype)


def merge_kernel(first_ref, second_ref, own_ref, back_ref, out_ref):
    for block in range(own_ref.shape[0] // QB):
        here = pl.ds(block * QB, QB)
        total = own_ref[here, :]
        for pick_ref in (first_ref, second_ref):
            pick = pick_ref[block]
            part = back_ref[jnp.maximum(pick, 0)].astype(jnp.float32)
            total += jnp.where(pick >= 0, part, 0.0)
        out_ref[here, :] = total.astype(out_ref.dtype)


def start_ctx(plan, me, peers, way, refs, outs, send_sem, recv_sem):
    for start in (True, False):
        for step in range(1, peers):
            target, origin = me + way * step, me - way * step

            @pl.when((target >= 0) & (target < peers))
            def _():
                for i, (ref, out) in enumerate(zip(refs, outs)):
                    copy = pltpu.make_async_remote_copy(
                        src_ref=ref.at[target],
                        dst_ref=out.at[me],
                        send_sem=send_sem.at[i, target],
                        recv_sem=recv_sem.at[i, me],
                        device_id={"ctx": target},
                        device_id_type=pl.DeviceIdType.MESH,
                    )
                    if start and plan != "wait":
                        copy.start()
                    if not start and plan != "start":
                        copy.wait_send()

            if not start and plan != "start":

                @pl.when((origin >= 0) & (origin < peers))
                def _():
                    for i, (ref, out) in enumerate(zip(refs, outs)):
                        pltpu.make_async_remote_copy(
                            src_ref=ref.at[origin],
                            dst_ref=out.at[origin],
                            send_sem=send_sem.at[i, origin],
                            recv_sem=recv_sem.at[i, origin],
                            device_id={"ctx": origin},
                            device_id_type=pl.DeviceIdType.MESH,
                        ).wait_recv()


def greet(axis, me, count, barrier):
    for step in range(1, count):
        pl.semaphore_signal(
            barrier,
            inc=1,
            device_id={axis: lax.rem(me + step, count)},
            device_id_type=pl.DeviceIdType.MESH,
        )


def send_kernel(peers, q_ref, g_ref, stat_ref, q_out, g_out, stat_out, send_sem, recv_sem):
    me = lax.axis_index("ctx")
    barrier = pltpu.get_barrier_semaphore()
    greet("ctx", me, peers, barrier)
    pl.semaphore_wait(barrier, peers - 1)
    start_ctx(
        "both", me, peers, -1, (stat_ref, q_ref, g_ref), (stat_out, q_out, g_out), send_sem, recv_sem
    )


def return_kernel(
    peers, shards, dq_ref, dk_ref, dv_ref, dq_out, dk_out, dv_out,
    send_sem, recv_sem, head_send, head_recv, local_sem,
):
    me, mine = lax.axis_index("ctx"), lax.axis_index("head")
    barrier = pltpu.get_barrier_semaphore()
    greet("ctx", me, peers, barrier)
    greet("head", mine, shards, barrier)
    pl.semaphore_wait(barrier, peers - 1 + shards - 1)
    pairs = ((dk_ref, dk_out), (dv_ref, dv_out))

    def head_copy(i, step):
        target = lax.rem(mine + step, shards)
        return pltpu.make_async_remote_copy(
            src_ref=pairs[i][0].at[target],
            dst_ref=pairs[i][1].at[mine],
            send_sem=head_send.at[i, step],
            recv_sem=head_recv.at[i, step],
            device_id={"head": target},
            device_id_type=pl.DeviceIdType.MESH,
        )

    start_ctx("start", me, peers, 1, (dq_ref,), (dq_out,), send_sem, recv_sem)
    for step in range(1, shards):
        for i in range(2):
            head_copy(i, step).start()
    keeps = [
        pltpu.make_async_copy(ref.at[mine], out.at[mine], local_sem.at[i])
        for i, (ref, out) in enumerate(pairs)
    ]
    for keep in keeps:
        keep.start()
    for keep in keeps:
        keep.wait()
    for step in range(1, shards):
        for i in range(2):
            copy = head_copy(i, step)
            copy.wait_send()
            copy.wait_recv()
    start_ctx("wait", me, peers, 1, (dq_ref,), (dq_out,), send_sem, recv_sem)


def body(queries, key_rows, value_rows, out_grad, outputs, logsumexp, selections):
    rows, kv, local, hd = queries.shape
    width = kv * local * hd
    heads = kv * local
    blocks = rows // QB
    peers = lax.axis_size("ctx")
    device = lax.axis_index("ctx")
    scale = hd ** (-0.5)
    f32, bf16 = jnp.float32, jnp.bfloat16
    params = pltpu.CompilerParams(vmem_limit_bytes=VMEM_LIMIT)

    q2 = queries.reshape(rows, width)
    g2 = out_grad.reshape(rows, width)
    k2 = key_rows.reshape(rows, kv * hd)
    v2 = value_rows.reshape(rows, kv * hd)
    lse = logsumexp.reshape(heads, rows)
    delta = jnp.transpose(
        jnp.sum((out_grad.astype(f32) * outputs.astype(f32)).reshape(rows, heads, hd), -1)
    )

    peer_ids = jnp.arange(peers, dtype=jnp.int32)
    block_ids = jnp.arange(blocks, dtype=jnp.int32)
    match = jnp.any(selections[:, 1:, None] == peer_ids, axis=1) & (peer_ids != device)
    live = jnp.any(match, axis=0)
    source = jnp.sum(jnp.where(match, block_ids[:, None], 0), axis=0)
    stats = jnp.concatenate([lse, delta], 0).reshape(2 * heads, blocks, QB).transpose(1, 0, 2)
    smem = pl.BlockSpec(memory_space=pltpu.SMEM)
    vmem = pl.BlockSpec(memory_space=pltpu.VMEM)
    q_blocks, g_blocks, send_stat = pl.pallas_call(
        pick_kernel,
        in_specs=[smem, smem, vmem, vmem, vmem],
        out_specs=[vmem] * 3,
        out_shape=[
            jax.ShapeDtypeStruct((peers, QB, width), bf16),
            jax.ShapeDtypeStruct((peers, QB, width), bf16),
            jax.ShapeDtypeStruct((peers, 3 * heads, QB), f32),
        ],
        compiler_params=params,
        name="pick",
    )(
        source,
        live.astype(jnp.int32),
        q2.reshape(blocks, QB, width),
        g2.reshape(blocks, QB, width),
        stats,
    )
    anywhere = pl.BlockSpec(memory_space=pl.ANY)
    dma = lambda *shape: pltpu.SemaphoreType.DMA(shape)
    like = lambda *arrays: [jax.ShapeDtypeStruct(x.shape, x.dtype) for x in arrays]
    got_q, got_g, got_stat = pl.pallas_call(
        functools.partial(send_kernel, peers),
        in_specs=[anywhere] * 3,
        out_specs=[anywhere] * 3,
        out_shape=like(q_blocks, g_blocks, send_stat),
        scratch_shapes=[dma(3, peers), dma(3, peers)],
        compiler_params=pltpu.CompilerParams(collective_id=0, has_side_effects=True),
        name="send",
    )(q_blocks, g_blocks, send_stat)
    got_q = got_q.reshape(peers * QB, width)
    got_g = got_g.reshape(peers * QB, width)

    column = lambda n: pl.BlockSpec((n, hd), lambda h, *_: (0, h))
    keys = pl.BlockSpec((rows, hd), lambda h, *_: (0, h // local))
    row = pl.BlockSpec((1, 1, rows), lambda h, *_: (h, 0, 0))
    own_q, own_k, own_v = pl.pallas_call(
        functools.partial(own_kernel, scale),
        grid=(heads,),
        in_specs=[column(rows), column(rows), keys, keys, row, row],
        out_specs=[column(rows)] * 3,
        out_shape=[jax.ShapeDtypeStruct((rows, width), f32)] * 3,
        compiler_params=params,
        name="own",
    )(q2, g2, k2, v2, lse.reshape(heads, 1, rows), delta.reshape(heads, 1, rows))

    marks = ((got_stat[:, 2 * heads, 0] > 0) & (peer_ids > device)).astype(jnp.int32)
    stacked = pl.BlockSpec((1, rows, hd), lambda h, *_: (h, 0, 0))
    dq_out, dk, dv = pl.pallas_call(
        functools.partial(slots_kernel, scale),
        grid_spec=pltpu.PrefetchScalarGridSpec(
            num_scalar_prefetch=1,
            grid=(heads,),
            in_specs=[
                column(peers * QB),
                column(peers * QB),
                pl.BlockSpec(got_stat.shape, lambda h, *_: (0, 0, 0)),
                keys,
                keys,
                column(rows),
                column(rows),
            ],
            out_specs=[column(peers * QB), stacked, stacked],
            scratch_shapes=[pltpu.VMEM((rows, hd), f32)] * 2,
        ),
        out_shape=[
            jax.ShapeDtypeStruct((peers * QB, width), bf16),
            jax.ShapeDtypeStruct((heads, rows, hd), bf16),
            jax.ShapeDtypeStruct((heads, rows, hd), bf16),
        ],
        compiler_params=params,
        name="slots",
    )(marks, got_q, got_g, got_stat, k2, v2, own_k, own_v)

    shards = lax.axis_size("head")
    dq_out = dq_out.reshape(peers, QB, width)
    dk = dk.reshape(shards, heads // shards, rows, hd)
    dv = dv.reshape(shards, heads // shards, rows, hd)
    back, dk, dv = pl.pallas_call(
        functools.partial(return_kernel, peers, shards),
        in_specs=[anywhere] * 3,
        out_specs=[anywhere] * 3,
        out_shape=like(dq_out, dk, dv),
        scratch_shapes=[
            dma(1, peers), dma(1, peers), dma(2, shards), dma(2, shards), dma(2),
        ],
        compiler_params=pltpu.CompilerParams(collective_id=1, has_side_effects=True),
        name="give_back",
    )(dq_out, dk, dv)

    def reduce_heads(part):
        part = part.reshape(shards, kv // shards, local, rows, hd)
        total = jnp.sum(part.astype(f32), axis=(0, 2))
        return jnp.transpose(total, (1, 0, 2)).astype(bf16)

    first, second = selections[:, 1], selections[:, 2]
    first = jnp.where(first != device, first, -1)
    second = jnp.where((second != device) & (second != first), second, -1)
    grad_q = pl.pallas_call(
        merge_kernel,
        in_specs=[smem, smem, vmem, vmem],
        out_specs=vmem,
        out_shape=jax.ShapeDtypeStruct((rows, width), bf16),
        compiler_params=params,
        name="merge",
    )(first, second, own_q, back)
    return (grad_q.reshape(rows, kv, local, hd), reduce_heads(dk), reduce_heads(dv))


def solution(mesh):
    in_specs = (
        P("ctx", None, "head", None),
        P("ctx", None, None),
        P("ctx", None, None),
        P("ctx", None, "head", None),
        P("ctx", None, "head", None),
        P(None, "head", "ctx"),
        P("ctx", None),
    )
    out_specs = (P("ctx", None, "head", None), P("ctx", "head", None), P("ctx", "head", None))
    return jax.shard_map(body, mesh=mesh, in_specs=in_specs, out_specs=out_specs, check_vma=False)
```

```python
import functools
import math

import jax
import jax.numpy as jnp
from jax import lax
from jax.experimental import pallas as pl
from jax.experimental.pallas import tpu as pltpu
from jax.sharding import PartitionSpec as P

QB = 128
TILE = 256
DEAD = 1e30
LOG2E = math.log2(math.e)
NT = (((1,), (1,)), ((), ()))
VMEM_LIMIT = 48 * 1024 * 1024


def dot(a, b, dims=(((1,), (0,)), ((), ()))):
    return lax.dot_general(a, b, dims, preferred_element_type=jnp.float32)


def piece(k, k_t, v, q, g, lse2, delta, scale, causal=False):
    p = jnp.exp2(dot(k, q, NT) * (scale * LOG2E) - lse2)
    if causal:
        keep = lax.broadcasted_iota(jnp.int32, p.shape, 0) <= lax.broadcasted_iota(
            jnp.int32, p.shape, 1
        )
        p = jnp.where(keep, p, 0.0)
    ds = (p * (dot(v, g, NT) - delta)).astype(jnp.bfloat16)
    return dot(k_t, ds), dot(ds, q), dot(p.astype(jnp.bfloat16), g)


def pick_kernel(source_ref, live_ref, q_ref, g_ref, stat_ref, q_out, g_out, stat_out):
    rows = stat_ref.shape[1]
    for peer in range(q_out.shape[0]):
        block = source_ref[peer]
        q_out[peer] = q_ref[block]
        g_out[peer] = g_ref[block]
        stat_out[peer, :rows] = stat_ref[block]
        live = live_ref[peer].astype(jnp.float32)
        stat_out[peer, rows:] = jnp.full((stat_out.shape[1] - rows, QB), live, jnp.float32)


def own_kernel(scale, q_ref, g_ref, k_ref, v_ref, lse_ref, delta_ref, dq_ref, dk_ref, dv_ref):
    rows = q_ref.shape[0]
    k_t = k_ref[...].T
    for lo in range(0, rows, TILE):
        here = pl.ds(lo, TILE)
        q, g = q_ref[here, :], g_ref[here, :]
        lse2, delta = lse_ref[0, :, here] * LOG2E, delta_ref[0, :, here]
        dq, dk, dv = piece(
            k_ref[here, :], k_t[:, lo : lo + TILE], v_ref[here, :], q, g, lse2, delta, scale, True
        )
        dk_ref[here, :] = dk
        dv_ref[here, :] = dv
        if lo:
            dq_more, dk, dv = piece(
                k_ref[:lo, :], k_t[:, :lo], v_ref[:lo, :], q, g, lse2, delta, scale
            )
            dq += dq_more
            dk_ref[:lo, :] += dk
            dv_ref[:lo, :] += dv
        dq_ref[here, :] = dq.T * scale


def slots_kernel(
    scale, mark_ref, q_ref, g_ref, stat_ref, k_ref, v_ref, dk_in, dv_in, dq_ref, dk_ref, dv_ref,
    acc_k, acc_v,
):
    head = pl.program_id(0)
    heads = pl.num_programs(0)
    k_t = k_ref[...].T
    acc_k[...] = dk_in[...]
    acc_v[...] = dv_in[...]
    for slot in range(q_ref.shape[0] // QB):
        here = pl.ds(slot * QB, QB)

        @pl.when(mark_ref[slot] > 0)
        def _():
            q, g = q_ref[here, :], g_ref[here, :]
            lse2 = stat_ref[slot, pl.ds(head, 1), :] * LOG2E
            delta = stat_ref[slot, pl.ds(heads + head, 1), :]
            dq, dk, dv = piece(k_ref[...], k_t, v_ref[...], q, g, lse2, delta, scale)
            acc_k[...] += dk
            acc_v[...] += dv
            dq_ref[here, :] = (dq.T * scale).astype(dq_ref.dtype)

        @pl.when(mark_ref[slot] <= 0)
        def _():
            dq_ref[here, :] = jnp.zeros((QB, q_ref.shape[1]), dq_ref.dtype)

    dk_ref[0] = (acc_k[...] * scale).astype(dk_ref.dtype)
    dv_ref[0] = acc_v[...].astype(dv_ref.dtype)


def merge_kernel(first_ref, second_ref, own_ref, back_ref, out_ref):
    for block in range(own_ref.shape[0] // QB):
        here = pl.ds(block * QB, QB)
        total = own_ref[here, :]
        for pick_ref in (first_ref, second_ref):
            pick = pick_ref[block]
            part = back_ref[jnp.maximum(pick, 0)].astype(jnp.float32)
            total += jnp.where(pick >= 0, part, 0.0)
        out_ref[here, :] = total.astype(out_ref.dtype)


def start_ctx(plan, me, peers, way, refs, outs, send_sem, recv_sem):
    for start in (True, False):
        for step in range(1, peers):
            target, origin = me + way * step, me - way * step

            @pl.when((target >= 0) & (target < peers))
            def _():
                for i, (ref, out) in enumerate(zip(refs, outs)):
                    copy = pltpu.make_async_remote_copy(
                        src_ref=ref.at[target],
                        dst_ref=out.at[me],
                        send_sem=send_sem.at[i, target],
                        recv_sem=recv_sem.at[i, me],
                        device_id={"ctx": target},
                        device_id_type=pl.DeviceIdType.MESH,
                    )
                    if start and plan != "wait":
                        copy.start()
                    if not start and plan != "start":
                        copy.wait_send()

            if not start and plan != "start":

                @pl.when((origin >= 0) & (origin < peers))
                def _():
                    for i, (ref, out) in enumerate(zip(refs, outs)):
                        pltpu.make_async_remote_copy(
                            src_ref=ref.at[origin],
                            dst_ref=out.at[origin],
                            send_sem=send_sem.at[i, origin],
                            recv_sem=recv_sem.at[i, origin],
                            device_id={"ctx": origin},
                            device_id_type=pl.DeviceIdType.MESH,
                        ).wait_recv()


def greet(axis, me, count, barrier):
    for step in range(1, count):
        pl.semaphore_signal(
            barrier,
            inc=1,
            device_id={axis: lax.rem(me + step, count)},
            device_id_type=pl.DeviceIdType.MESH,
        )


def send_kernel(
    peers, scale, q_ref, g_ref, stat_ref, q_own, g_own, k_ref, v_ref, lse_ref, delta_ref,
    q_out, g_out, stat_out, dq_ref, dk_ref, dv_ref, send_sem, recv_sem,
):
    me = lax.axis_index("ctx")
    barrier = pltpu.get_barrier_semaphore()
    greet("ctx", me, peers, barrier)
    pl.semaphore_wait(barrier, peers - 1)
    sent, outs = (stat_ref, q_ref, g_ref), (stat_out, q_out, g_out)
    start_ctx("start", me, peers, -1, sent, outs, send_sem, recv_sem)
    heads = lse_ref.shape[0]
    hd = q_own.shape[1] // heads
    local = q_own.shape[1] // k_ref.shape[1]

    def one_head(head, carry):
        at = (slice(None), pl.ds(pl.multiple_of(head * hd, hd), hd))
        key_at = (slice(None), pl.ds(pl.multiple_of(head // local * hd, hd), hd))
        row = pl.ds(head, 1)
        own_kernel(
            scale, q_own.at[at], g_own.at[at], k_ref.at[key_at], v_ref.at[key_at],
            lse_ref.at[row], delta_ref.at[row], dq_ref.at[at], dk_ref.at[at], dv_ref.at[at],
        )
        return carry

    lax.fori_loop(0, heads, one_head, 0)
    start_ctx("wait", me, peers, -1, sent, outs, send_sem, recv_sem)


def return_kernel(
    peers, shards, dq_ref, dk_ref, dv_ref, dq_out, dk_out, dv_out,
    send_sem, recv_sem, head_send, head_recv, local_sem,
):
    me, mine = lax.axis_index("ctx"), lax.axis_index("head")
    barrier = pltpu.get_barrier_semaphore()
    greet("ctx", me, peers, barrier)
    greet("head", mine, shards, barrier)
    pl.semaphore_wait(barrier, peers - 1 + shards - 1)
    pairs = ((dk_ref, dk_out), (dv_ref, dv_out))

    def head_copy(i, step):
        target = lax.rem(mine + step, shards)
        return pltpu.make_async_remote_copy(
            src_ref=pairs[i][0].at[target],
            dst_ref=pairs[i][1].at[mine],
            send_sem=head_send.at[i, step],
            recv_sem=head_recv.at[i, step],
            device_id={"head": target},
            device_id_type=pl.DeviceIdType.MESH,
        )

    start_ctx("start", me, peers, 1, (dq_ref,), (dq_out,), send_sem, recv_sem)
    for step in range(1, shards):
        for i in range(2):
            head_copy(i, step).start()
    keeps = [
        pltpu.make_async_copy(ref.at[mine], out.at[mine], local_sem.at[i])
        for i, (ref, out) in enumerate(pairs)
    ]
    for keep in keeps:
        keep.start()
    for keep in keeps:
        keep.wait()
    for step in range(1, shards):
        for i in range(2):
            copy = head_copy(i, step)
            copy.wait_send()
            copy.wait_recv()
    start_ctx("wait", me, peers, 1, (dq_ref,), (dq_out,), send_sem, recv_sem)


def body(queries, key_rows, value_rows, out_grad, outputs, logsumexp, selections):
    rows, kv, local, hd = queries.shape
    width = kv * local * hd
    heads = kv * local
    blocks = rows // QB
    peers = lax.axis_size("ctx")
    device = lax.axis_index("ctx")
    scale = hd ** (-0.5)
    f32, bf16 = jnp.float32, jnp.bfloat16
    params = pltpu.CompilerParams(vmem_limit_bytes=VMEM_LIMIT)

    q2 = queries.reshape(rows, width)
    g2 = out_grad.reshape(rows, width)
    k2 = key_rows.reshape(rows, kv * hd)
    v2 = value_rows.reshape(rows, kv * hd)
    lse = logsumexp.reshape(heads, rows)
    delta = jnp.transpose(
        jnp.sum((out_grad.astype(f32) * outputs.astype(f32)).reshape(rows, heads, hd), -1)
    )

    peer_ids = jnp.arange(peers, dtype=jnp.int32)
    block_ids = jnp.arange(blocks, dtype=jnp.int32)
    match = jnp.any(selections[:, 1:, None] == peer_ids, axis=1) & (peer_ids != device)
    live = jnp.any(match, axis=0)
    source = jnp.sum(jnp.where(match, block_ids[:, None], 0), axis=0)
    stats = jnp.concatenate([lse, delta], 0).reshape(2 * heads, blocks, QB).transpose(1, 0, 2)
    smem = pl.BlockSpec(memory_space=pltpu.SMEM)
    vmem = pl.BlockSpec(memory_space=pltpu.VMEM)
    q_blocks, g_blocks, send_stat = pl.pallas_call(
        pick_kernel,
        in_specs=[smem, smem, vmem, vmem, vmem],
        out_specs=[vmem] * 3,
        out_shape=[
            jax.ShapeDtypeStruct((peers, QB, width), bf16),
            jax.ShapeDtypeStruct((peers, QB, width), bf16),
            jax.ShapeDtypeStruct((peers, 3 * heads, QB), f32),
        ],
        compiler_params=params,
        name="pick",
    )(
        source,
        live.astype(jnp.int32),
        q2.reshape(blocks, QB, width),
        g2.reshape(blocks, QB, width),
        stats,
    )
    anywhere = pl.BlockSpec(memory_space=pl.ANY)
    dma = lambda *shape: pltpu.SemaphoreType.DMA(shape)
    like = lambda *arrays: [jax.ShapeDtypeStruct(x.shape, x.dtype) for x in arrays]
    own_shape = [jax.ShapeDtypeStruct((rows, width), f32)] * 3
    got_q, got_g, got_stat, own_q, own_k, own_v = pl.pallas_call(
        functools.partial(send_kernel, peers, scale),
        in_specs=[anywhere] * 3 + [vmem] * 6,
        out_specs=[anywhere] * 3 + [vmem] * 3,
        out_shape=like(q_blocks, g_blocks, send_stat) + own_shape,
        scratch_shapes=[dma(3, peers), dma(3, peers)],
        compiler_params=pltpu.CompilerParams(
            collective_id=0, has_side_effects=True, vmem_limit_bytes=VMEM_LIMIT
        ),
        name="send",
    )(
        q_blocks, g_blocks, send_stat, q2, g2, k2, v2,
        lse.reshape(heads, 1, rows), delta.reshape(heads, 1, rows),
    )
    got_q = got_q.reshape(peers * QB, width)
    got_g = got_g.reshape(peers * QB, width)

    column = lambda n: pl.BlockSpec((n, hd), lambda h, *_: (0, h))
    keys = pl.BlockSpec((rows, hd), lambda h, *_: (0, h // local))

    marks = ((got_stat[:, 2 * heads, 0] > 0) & (peer_ids > device)).astype(jnp.int32)
    stacked = pl.BlockSpec((1, rows, hd), lambda h, *_: (h, 0, 0))
    dq_out, dk, dv = pl.pallas_call(
        functools.partial(slots_kernel, scale),
        grid_spec=pltpu.PrefetchScalarGridSpec(
            num_scalar_prefetch=1,
            grid=(heads,),
            in_specs=[
                column(peers * QB),
                column(peers * QB),
                pl.BlockSpec(got_stat.shape, lambda h, *_: (0, 0, 0)),
                keys,
                keys,
                column(rows),
                column(rows),
            ],
            out_specs=[column(peers * QB), stacked, stacked],
            scratch_shapes=[pltpu.VMEM((rows, hd), f32)] * 2,
        ),
        out_shape=[
            jax.ShapeDtypeStruct((peers * QB, width), bf16),
            jax.ShapeDtypeStruct((heads, rows, hd), bf16),
            jax.ShapeDtypeStruct((heads, rows, hd), bf16),
        ],
        compiler_params=params,
        name="slots",
    )(marks, got_q, got_g, got_stat, k2, v2, own_k, own_v)

    shards = lax.axis_size("head")
    dq_out = dq_out.reshape(peers, QB, width)
    dk = dk.reshape(shards, heads // shards, rows, hd)
    dv = dv.reshape(shards, heads // shards, rows, hd)
    back, dk, dv = pl.pallas_call(
        functools.partial(return_kernel, peers, shards),
        in_specs=[anywhere] * 3,
        out_specs=[anywhere] * 3,
        out_shape=like(dq_out, dk, dv),
        scratch_shapes=[
            dma(1, peers), dma(1, peers), dma(2, shards), dma(2, shards), dma(2),
        ],
        compiler_params=pltpu.CompilerParams(collective_id=1, has_side_effects=True),
        name="give_back",
    )(dq_out, dk, dv)

    def reduce_heads(part):
        part = part.reshape(shards, kv // shards, local, rows, hd)
        total = jnp.sum(part.astype(f32), axis=(0, 2))
        return jnp.transpose(total, (1, 0, 2)).astype(bf16)

    first, second = selections[:, 1], selections[:, 2]
    first = jnp.where(first != device, first, -1)
    second = jnp.where((second != device) & (second != first), second, -1)
    grad_q = pl.pallas_call(
        merge_kernel,
        in_specs=[smem, smem, vmem, vmem],
        out_specs=vmem,
        out_shape=jax.ShapeDtypeStruct((rows, width), bf16),
        compiler_params=params,
        name="merge",
    )(first, second, own_q, back)
    return (grad_q.reshape(rows, kv, local, hd), reduce_heads(dk), reduce_heads(dv))


def solution(mesh):
    in_specs = (
        P("ctx", None, "head", None),
        P("ctx", None, None),
        P("ctx", None, None),
        P("ctx", None, "head", None),
        P("ctx", None, "head", None),
        P(None, "head", "ctx"),
        P("ctx", None),
    )
    out_specs = (P("ctx", None, "head", None), P("ctx", "head", None), P("ctx", "head", None))
    return jax.shard_map(body, mesh=mesh, in_specs=in_specs, out_specs=out_specs, check_vma=False)
```

```python
import functools
import math

import jax
import jax.numpy as jnp
from jax import lax
from jax.experimental import pallas as pl
from jax.experimental.pallas import tpu as pltpu
from jax.sharding import PartitionSpec as P

QB = 128
TILE = 256
DEAD = 1e30
LOG2E = math.log2(math.e)
NT = (((1,), (1,)), ((), ()))
VMEM_LIMIT = 48 * 1024 * 1024


def dot(a, b, dims=(((1,), (0,)), ((), ()))):
    return lax.dot_general(a, b, dims, preferred_element_type=jnp.float32)


def piece(k, k_t, v, q, g, lse2, delta, scale, causal=False):
    p = jnp.exp2(dot(k, q, NT) * (scale * LOG2E) - lse2)
    if causal:
        keep = lax.broadcasted_iota(jnp.int32, p.shape, 0) <= lax.broadcasted_iota(
            jnp.int32, p.shape, 1
        )
        p = jnp.where(keep, p, 0.0)
    ds = (p * (dot(v, g, NT) - delta)).astype(jnp.bfloat16)
    return dot(k_t, ds), dot(ds, q), dot(p.astype(jnp.bfloat16), g)


def pick_kernel(source_ref, live_ref, q_ref, g_ref, stat_ref, q_out, g_out, stat_out):
    rows = stat_ref.shape[1]
    for peer in range(q_out.shape[0]):
        block = source_ref[peer]
        q_out[peer] = q_ref[block]
        g_out[peer] = g_ref[block]
        stat_out[peer, :rows] = stat_ref[block]
        live = live_ref[peer].astype(jnp.float32)
        stat_out[peer, rows:] = jnp.full((stat_out.shape[1] - rows, QB), live, jnp.float32)


def own_kernel(scale, q_ref, g_ref, k_ref, v_ref, lse_ref, delta_ref, dq_ref, dk_ref, dv_ref):
    rows = q_ref.shape[0]
    k_t = k_ref[...].T
    for lo in range(0, rows, TILE):
        here = pl.ds(lo, TILE)
        q, g = q_ref[here, :], g_ref[here, :]
        lse2, delta = lse_ref[0, :, here] * LOG2E, delta_ref[0, :, here]
        dq, dk, dv = piece(
            k_ref[here, :], k_t[:, lo : lo + TILE], v_ref[here, :], q, g, lse2, delta, scale, True
        )
        dk_ref[here, :] = dk
        dv_ref[here, :] = dv
        if lo:
            dq_more, dk, dv = piece(
                k_ref[:lo, :], k_t[:, :lo], v_ref[:lo, :], q, g, lse2, delta, scale
            )
            dq += dq_more
            dk_ref[:lo, :] += dk
            dv_ref[:lo, :] += dv
        dq_ref[here, :] = dq.T * scale


def merge_kernel(first_ref, second_ref, own_ref, back_ref, out_ref):
    for block in range(own_ref.shape[0] // QB):
        here = pl.ds(block * QB, QB)
        total = own_ref[here, :]
        for pick_ref in (first_ref, second_ref):
            pick = pick_ref[block]
            part = back_ref[jnp.maximum(pick, 0)].astype(jnp.float32)
            total += jnp.where(pick >= 0, part, 0.0)
        out_ref[here, :] = total.astype(out_ref.dtype)


def start_ctx(plan, me, peers, way, refs, outs, send_sem, recv_sem):
    for start in (True, False):
        for step in range(1, peers):
            target, origin = me + way * step, me - way * step

            @pl.when((target >= 0) & (target < peers))
            def _():
                for i, (ref, out) in enumerate(zip(refs, outs)):
                    copy = pltpu.make_async_remote_copy(
                        src_ref=ref.at[target],
                        dst_ref=out.at[me],
                        send_sem=send_sem.at[i, target],
                        recv_sem=recv_sem.at[i, me],
                        device_id={"ctx": target},
                        device_id_type=pl.DeviceIdType.MESH,
                    )
                    if start and plan in ("start", "both"):
                        copy.start()
                    if not start and plan != "start":
                        copy.wait_send()

            if not start and plan in ("wait", "both"):

                @pl.when((origin >= 0) & (origin < peers))
                def _():
                    for i, (ref, out) in enumerate(zip(refs, outs)):
                        pltpu.make_async_remote_copy(
                            src_ref=ref.at[origin],
                            dst_ref=out.at[origin],
                            send_sem=send_sem.at[i, origin],
                            recv_sem=recv_sem.at[i, origin],
                            device_id={"ctx": origin},
                            device_id_type=pl.DeviceIdType.MESH,
                        ).wait_recv()


def greet(axis, me, count, barrier):
    for step in range(1, count):
        pl.semaphore_signal(
            barrier,
            inc=1,
            device_id={axis: lax.rem(me + step, count)},
            device_id_type=pl.DeviceIdType.MESH,
        )


def send_kernel(
    peers, scale, q_ref, g_ref, stat_ref, q_own, g_own, k_ref, v_ref, lse_ref, delta_ref,
    q_out, g_out, stat_out, dq_ref, slot_ref, dk_out, dv_out,
    dk_ref, dv_ref, kt_ref, send_sem, recv_sem,
):
    me = lax.axis_index("ctx")
    barrier = pltpu.get_barrier_semaphore()
    greet("ctx", me, peers, barrier)
    pl.semaphore_wait(barrier, peers - 1)
    sent, outs = (stat_ref, q_ref, g_ref), (stat_out, q_out, g_out)
    start_ctx("start", me, peers, -1, sent, outs, send_sem, recv_sem)
    heads = lse_ref.shape[0]
    hd = q_own.shape[1] // heads
    local = q_own.shape[1] // k_ref.shape[1]

    def one_head(head, carry):
        at = (slice(None), pl.ds(pl.multiple_of(head * hd, hd), hd))
        key_at = (slice(None), pl.ds(pl.multiple_of(head // local * hd, hd), hd))
        row = pl.ds(head, 1)
        own_kernel(
            scale, q_own.at[at], g_own.at[at], k_ref.at[key_at], v_ref.at[key_at],
            lse_ref.at[row], delta_ref.at[row], dq_ref.at[at], dk_ref.at[at], dv_ref.at[at],
        )
        return carry

    lax.fori_loop(0, heads, one_head, 0)

    def turn_keys(head, carry):
        at = pl.ds(pl.multiple_of(head * hd, hd), hd)
        kt_ref[at, :] = k_ref[:, at].T
        return carry

    lax.fori_loop(0, heads // local, turn_keys, 0)

    def one_slot(step, carry):
        origin = me + step

        @pl.when(origin < peers)
        def _():
            for i, (ref, out) in enumerate(zip(sent, outs)):
                pltpu.make_async_remote_copy(
                    src_ref=ref.at[origin],
                    dst_ref=out.at[origin],
                    send_sem=send_sem.at[i, origin],
                    recv_sem=recv_sem.at[i, origin],
                    device_id={"ctx": origin},
                    device_id_type=pl.DeviceIdType.MESH,
                ).wait_recv()

            def slot_head(head, inner):
                at = pl.ds(pl.multiple_of(head * hd, hd), hd)
                key_at = pl.ds(pl.multiple_of(head // local * hd, hd), hd)
                live = stat_out[origin, pl.ds(2 * heads, 1), :] > 0
                lse2 = jnp.where(live, stat_out[origin, pl.ds(head, 1), :] * LOG2E, DEAD)
                delta = stat_out[origin, pl.ds(heads + head, 1), :]
                dq, dk, dv = piece(
                    k_ref[:, key_at], kt_ref[key_at, :], v_ref[:, key_at],
                    q_out[origin, :, at], g_out[origin, :, at], lse2, delta, scale,
                )
                dk_ref[:, at] += dk
                dv_ref[:, at] += dv
                slot_ref[origin, :, at] = (dq.T * scale).astype(slot_ref.dtype)
                return inner

            lax.fori_loop(0, heads, slot_head, 0)

        return carry

    lax.fori_loop(1, peers, one_slot, 0)
    for head in range(heads):
        at = slice(head * hd, head * hd + hd)
        dk_out[head] = (dk_ref[:, at] * scale).astype(dk_out.dtype)
        dv_out[head] = dv_ref[:, at].astype(dv_out.dtype)
    start_ctx("sends", me, peers, -1, sent, outs, send_sem, recv_sem)


def return_kernel(
    peers, shards, dq_ref, dk_ref, dv_ref, dq_out, dk_out, dv_out,
    send_sem, recv_sem, head_send, head_recv, local_sem,
):
    me, mine = lax.axis_index("ctx"), lax.axis_index("head")
    barrier = pltpu.get_barrier_semaphore()
    greet("ctx", me, peers, barrier)
    greet("head", mine, shards, barrier)
    pl.semaphore_wait(barrier, peers - 1 + shards - 1)
    pairs = ((dk_ref, dk_out), (dv_ref, dv_out))

    def head_copy(i, step):
        target = lax.rem(mine + step, shards)
        return pltpu.make_async_remote_copy(
            src_ref=pairs[i][0].at[target],
            dst_ref=pairs[i][1].at[mine],
            send_sem=head_send.at[i, step],
            recv_sem=head_recv.at[i, step],
            device_id={"head": target},
            device_id_type=pl.DeviceIdType.MESH,
        )

    start_ctx("start", me, peers, 1, (dq_ref,), (dq_out,), send_sem, recv_sem)
    for step in range(1, shards):
        for i in range(2):
            head_copy(i, step).start()
    keeps = [
        pltpu.make_async_copy(ref.at[mine], out.at[mine], local_sem.at[i])
        for i, (ref, out) in enumerate(pairs)
    ]
    for keep in keeps:
        keep.start()
    for keep in keeps:
        keep.wait()
    for step in range(1, shards):
        for i in range(2):
            copy = head_copy(i, step)
            copy.wait_send()
            copy.wait_recv()
    start_ctx("wait", me, peers, 1, (dq_ref,), (dq_out,), send_sem, recv_sem)


def body(queries, key_rows, value_rows, out_grad, outputs, logsumexp, selections):
    rows, kv, local, hd = queries.shape
    width = kv * local * hd
    heads = kv * local
    blocks = rows // QB
    peers = lax.axis_size("ctx")
    device = lax.axis_index("ctx")
    scale = hd ** (-0.5)
    f32, bf16 = jnp.float32, jnp.bfloat16
    params = pltpu.CompilerParams(vmem_limit_bytes=VMEM_LIMIT)

    q2 = queries.reshape(rows, width)
    g2 = out_grad.reshape(rows, width)
    k2 = key_rows.reshape(rows, kv * hd)
    v2 = value_rows.reshape(rows, kv * hd)
    lse = logsumexp.reshape(heads, rows)
    delta = jnp.transpose(
        jnp.sum((out_grad.astype(f32) * outputs.astype(f32)).reshape(rows, heads, hd), -1)
    )

    peer_ids = jnp.arange(peers, dtype=jnp.int32)
    block_ids = jnp.arange(blocks, dtype=jnp.int32)
    match = jnp.any(selections[:, 1:, None] == peer_ids, axis=1) & (peer_ids != device)
    live = jnp.any(match, axis=0)
    source = jnp.sum(jnp.where(match, block_ids[:, None], 0), axis=0)
    stats = jnp.concatenate([lse, delta], 0).reshape(2 * heads, blocks, QB).transpose(1, 0, 2)
    smem = pl.BlockSpec(memory_space=pltpu.SMEM)
    vmem = pl.BlockSpec(memory_space=pltpu.VMEM)
    q_blocks, g_blocks, send_stat = pl.pallas_call(
        pick_kernel,
        in_specs=[smem, smem, vmem, vmem, vmem],
        out_specs=[vmem] * 3,
        out_shape=[
            jax.ShapeDtypeStruct((peers, QB, width), bf16),
            jax.ShapeDtypeStruct((peers, QB, width), bf16),
            jax.ShapeDtypeStruct((peers, 3 * heads, QB), f32),
        ],
        compiler_params=params,
        name="pick",
    )(
        source,
        live.astype(jnp.int32),
        q2.reshape(blocks, QB, width),
        g2.reshape(blocks, QB, width),
        stats,
    )
    anywhere = pl.BlockSpec(memory_space=pl.ANY)
    dma = lambda *shape: pltpu.SemaphoreType.DMA(shape)
    like = lambda *arrays: [jax.ShapeDtypeStruct(x.shape, x.dtype) for x in arrays]
    grads = jax.ShapeDtypeStruct((heads, rows, hd), bf16)
    _, _, _, own_q, dq_out, dk, dv = pl.pallas_call(
        functools.partial(send_kernel, peers, scale),
        in_specs=[anywhere] * 3 + [vmem] * 6,
        out_specs=[vmem] * 7,
        out_shape=like(q_blocks, g_blocks, send_stat)
        + [jax.ShapeDtypeStruct((rows, width), f32)]
        + like(q_blocks)
        + [grads, grads],
        scratch_shapes=[
            pltpu.VMEM((rows, width), f32),
            pltpu.VMEM((rows, width), f32),
            pltpu.VMEM((kv * hd, rows), bf16),
            dma(3, peers),
            dma(3, peers),
        ],
        compiler_params=pltpu.CompilerParams(
            collective_id=0, has_side_effects=True, vmem_limit_bytes=VMEM_LIMIT
        ),
        name="send",
    )(
        q_blocks, g_blocks, send_stat, q2, g2, k2, v2,
        lse.reshape(heads, 1, rows), delta.reshape(heads, 1, rows),
    )

    shards = lax.axis_size("head")
    dk = dk.reshape(shards, heads // shards, rows, hd)
    dv = dv.reshape(shards, heads // shards, rows, hd)
    back, dk, dv = pl.pallas_call(
        functools.partial(return_kernel, peers, shards),
        in_specs=[anywhere] * 3,
        out_specs=[anywhere] * 3,
        out_shape=like(dq_out, dk, dv),
        scratch_shapes=[
            dma(1, peers), dma(1, peers), dma(2, shards), dma(2, shards), dma(2),
        ],
        compiler_params=pltpu.CompilerParams(collective_id=1, has_side_effects=True),
        name="give_back",
    )(dq_out, dk, dv)

    def reduce_heads(part):
        part = part.reshape(shards, kv // shards, local, rows, hd)
        total = jnp.sum(part.astype(f32), axis=(0, 2))
        return jnp.transpose(total, (1, 0, 2)).astype(bf16)

    first, second = selections[:, 1], selections[:, 2]
    first = jnp.where(first != device, first, -1)
    second = jnp.where((second != device) & (second != first), second, -1)
    grad_q = pl.pallas_call(
        merge_kernel,
        in_specs=[smem, smem, vmem, vmem],
        out_specs=vmem,
        out_shape=jax.ShapeDtypeStruct((rows, width), bf16),
        compiler_params=params,
        name="merge",
    )(first, second, own_q, back)
    return (grad_q.reshape(rows, kv, local, hd), reduce_heads(dk), reduce_heads(dv))


def solution(mesh):
    in_specs = (
        P("ctx", None, "head", None),
        P("ctx", None, None),
        P("ctx", None, None),
        P("ctx", None, "head", None),
        P("ctx", None, "head", None),
        P(None, "head", "ctx"),
        P("ctx", None),
    )
    out_specs = (P("ctx", None, "head", None), P("ctx", "head", None), P("ctx", "head", None))
    return jax.shard_map(body, mesh=mesh, in_specs=in_specs, out_specs=out_specs, check_vma=False)
```
